256 devices in a mesh: row: 8 (over x, core), col: 32 (over y, z).
Axes of the slice: x: 4, y: 4, z: 8, core: 2. Of those that a mesh axis runs over, the one named last changes fastest.
Arguments:
- grad: bfloat16 [1024, 73728], P('row', 'col'), may hold values from -180 to 180
- weight: bfloat16 [1024, 73728], P('row', 'col'), may hold values from -6 to 6
- residual: bfloat16 [1024, 73728], P('row', 'col'), may hold values from -0.0038909912 to 0.0038909912
- row_state: float32 [1024], P('row'), may hold values from 0.01 to 0.5
- col_state: float32 [73728], P('col'), may hold values from 0.01 to 0.5
- out_grad: bfloat16 [2048, 73728], P('col'), may hold values from -0.0234375 to 0.0234375
Outputs:
- new_weight: bfloat16 [1024, 73728], P('row', 'col')
- row_out: float32 [1024], P('row')
- col_out: float32 [73728], P('col')
- input_grad: bfloat16 [2048, 1024], P('col', 'row')
The draws below stay inside these ranges and needn't reach their ends.
All inputs are finite; a program needn't handle non-finite values.
Results may differ from the reference program's by a relative error of at most 0.0014.
The reference program's roundings to bfloat16 on the way count: a program that leaves them out, or rounds other values in their place, can miss the bound.
Values may be sent and summed in bfloat16 or wider, within the bound.
No kernel may reach another device: no remote copies, remote signals or barrier semaphores. Data moves between devices by JAX's collectives and lax.ppermute only.
A program may use at most 128 MiB of HBM per device.

```python
import math
import jax
import jax.numpy as jnp
from jax import lax

FF = 73728
ROWS = 1024
TOKENS = 2048


def draw_grad(key, part):
    key = jax.random.fold_in(key, 7)
    first, second, third, fourth = jax.random.split(key, 4)
    base = jnp.clip(jax.random.normal(first, (ROWS, FF), jnp.float32), -6.0, 6.0)
    row_scale = jnp.exp(jax.random.uniform(second, (ROWS, 1), jnp.float32, 0.0, math.log(10.0)))
    col_scale = jnp.exp(jax.random.uniform(third, (1, FF), jnp.float32, 0.0, math.log(10.0)))
    row_trend = jnp.exp(math.log(3.0) * jnp.arange(ROWS, dtype=jnp.float32) / ROWS)[:, None]
    col_trend = jnp.exp(math.log(3.0) * jnp.arange(FF, dtype=jnp.float32) / FF)[None, :]
    grid = jnp.exp(2.0 * jax.random.uniform(fourth, (8, 16), jnp.float32, -1.0, 1.0))
    row_block = jnp.arange(ROWS, dtype=jnp.int32) * 8 // ROWS
    col_block = jnp.arange(FF, dtype=jnp.int32) * 16 // FF
    block_factor = jnp.take(jnp.take(grid, row_block, axis=0), col_block, axis=1)
    values = base * row_scale * col_scale * row_trend * col_trend * block_factor / (30.0 * math.e)
    return jnp.clip(values, -180.0, 180.0).astype(jnp.bfloat16)


def block_levels(stream_key, dims, cuts, low, high):
    gain = 1.0
    for dim, parts in cuts:
        draws = jax.random.uniform(jax.random.fold_in(jax.random.fold_in(stream_key, 6), dim), (parts,), jnp.float32, low / len(cuts), high / len(cuts))
        gain = gain * jnp.repeat(jnp.exp(draws), dims[dim] // parts).reshape((-1,) + (1,) * (len(dims) - 1 - dim))
    return gain


def scatter_about(own_key, shape, scale, reach, cuts=(), kind=jnp.bfloat16):
    array = jax.random.normal(own_key, shape, jnp.float32) * scale
    if len(cuts) > 0:
        array = block_levels(own_key, shape, cuts, -0.22, 0.18) * array
    return jnp.clip(array, min=-reach, max=reach).astype(kind)


def setup_inputs(seed: int = 0) -> dict:
    keys = jax.random.split(jax.random.key(seed), 7)
    grad = draw_grad(jax.random.fold_in(keys[6], 71), 0)
    weight = scatter_about(keys[1], (ROWS, FF), 1.0, 6.0, ((0, 8), (1, 32)))
    residual = jnp.clip(jax.random.uniform(keys[2], (ROWS, FF), jnp.float32, -0.0038909912, 0.0038909912) * block_levels(keys[2], (ROWS, FF), ((0, 8), (1, 32)), -0.4, 0.0), -0.0038909912, 0.0038909912).astype(jnp.bfloat16)
    row_state = jnp.clip(jnp.exp(math.log(0.5) - 3.912023 * jax.random.uniform(keys[3], (ROWS,), jnp.float32) ** block_levels(keys[3], (ROWS,), ((0, 8),), -0.2, 0.2)), 0.01, 0.5)
    col_state = jnp.clip(jnp.exp(math.log(0.5) - 3.912023 * jax.random.uniform(keys[4], (FF,), jnp.float32) ** block_levels(keys[4], (FF,), ((0, 32),), -0.2, 0.2)), 0.01, 0.5)
    out_grad = scatter_about(keys[5], (TOKENS, FF), FF ** -0.5, 0.0234375, ((0, 32),))
    return dict(grad=grad, weight=weight, residual=residual, row_state=row_state, col_state=col_state, out_grad=out_grad)


decay_rate = 0.9
step_size = 0.05
clip_level = 1.0
tiny_square = 1e-30

def reference(grad, weight, residual, row_state, col_state, out_grad):
    grad_full = grad.astype(jnp.float32)
    squares = grad_full * grad_full + tiny_square
    row_out = decay_rate * row_state + (1.0 - decay_rate) * lax.optimization_barrier(jnp.sum(squares, axis=1)) / FF
    col_out = decay_rate * col_state + (1.0 - decay_rate) * lax.optimization_barrier(jnp.sum(squares, axis=0)) / ROWS
    scaled = grad_full * lax.rsqrt(row_out[:, None] * col_out[None, :])
    master = weight.astype(jnp.float32) + residual.astype(jnp.float32)
    entries = ROWS * FF
    upd_rms = jnp.sqrt(jnp.sum(scaled * scaled) / entries)
    w_rms = jnp.sqrt(jnp.sum(master * master) / entries)
    factor = step_size * w_rms / jnp.maximum(1.0, upd_rms / clip_level)
    full = master - factor * scaled
    new_weight = full.astype(jnp.bfloat16)
    input_grad = lax.dot_general(out_grad, new_weight, (((1,), (1,)), ((), ())), preferred_element_type=jnp.float32).astype(jnp.bfloat16)
    return (new_weight, row_out, col_out, input_grad)
```

```python
import jax
import jax.numpy as jnp
from jax import lax
from jax.sharding import Mesh, PartitionSpec as P

decay_rate = 0.9
step_size = 0.05
clip_level = 1.0
tiny_square = 1e-30
ROW = ("x", "core")
COL = ("y", "z")


def spread_sum(value, axes, count):
    copies = jnp.broadcast_to(value[None], (count,) + value.shape)
    return jnp.sum(lax.all_to_all(copies, axes, 0, 0, tiled=True), axis=0)


def body(grad, weight, residual, row_state, col_state, out_grad):
    rows, cols = grad.shape
    tokens = out_grad.shape[0]
    n_row, n_y, n_z = lax.axis_size(ROW), lax.axis_size("y"), lax.axis_size("z")
    n_col = n_y * n_z
    all_rows, all_cols = rows * n_row, cols * n_col
    part = tokens // n_row

    me = lax.axis_index(ROW)
    share = lax.dynamic_slice_in_dim(out_grad, me * part, part, 0)
    share = share.reshape(part, n_y, n_z, cols).transpose(2, 1, 0, 3)
    share = lax.all_to_all(share, "z", 0, 0, tiled=True)
    tokens_in = lax.all_gather(share, ROW, axis=0)

    grad_full = grad.astype(jnp.float32)
    squares = grad_full * grad_full + tiny_square
    col_part = jnp.sum(squares, axis=0).reshape(cols // 128, 128)
    col_total = spread_sum(col_part, ROW, n_row).reshape(cols)
    col_out = decay_rate * col_state + (1.0 - decay_rate) * col_total / all_rows
    master = weight.astype(jnp.float32) + residual.astype(jnp.float32)
    row_part = jnp.sum(squares, axis=1)
    scaled_part = jnp.sum(grad_full * grad_full * (1.0 / col_out)[None, :], axis=1)
    w_part = jnp.sum(master * master, axis=1)
    sums = jnp.concatenate([row_part[None], scaled_part[None], w_part[None], jnp.zeros((5, rows), jnp.float32)])
    sums = spread_sum(sums, COL, n_col)
    row_out = decay_rate * row_state + (1.0 - decay_rate) * sums[0] / all_cols
    upd_part = jnp.sum(sums[1] / row_out)
    w_part = jnp.sum(sums[2])
    pair = jnp.concatenate([jnp.full((4, 128), upd_part), jnp.full((4, 128), w_part)])
    pair = spread_sum(pair, ROW, n_row)
    entries = all_rows * all_cols
    upd_rms = jnp.sqrt(pair[0, 0] / entries)
    w_rms = jnp.sqrt(pair[4, 0] / entries)
    factor = step_size * w_rms / jnp.maximum(1.0, upd_rms / clip_level)
    scaled = grad_full * lax.rsqrt(row_out[:, None] * col_out[None, :])
    new_weight = (master - factor * scaled).astype(jnp.bfloat16)
    around = lax.all_gather(new_weight, "y", axis=0)

    total = 0.0
    for i in range(n_y):
        total += lax.dot_general(tokens_in[:, :, i], around[i], (((3,), (1,)), ((), ())), preferred_element_type=jnp.float32)
    total = total.transpose(1, 0, 2, 3).reshape(n_z, tokens, rows)
    total = lax.all_to_all(total, "z", 0, 0, tiled=True)
    input_grad = jnp.sum(total, axis=0).astype(jnp.bfloat16)
    return (new_weight, row_out, col_out, input_grad)


def solution(mesh):
    fine = Mesh(mesh.devices.reshape(4, 2, 4, 8), ("x", "core", "y", "z"))
    in_specs = (P(ROW, COL), P(ROW, COL), P(ROW, COL), P(ROW), P(COL), P(COL, None))
    out_specs = (P(ROW, COL), P(ROW), P(COL), P(COL, ROW))
    return jax.shard_map(body, mesh=fine, in_specs=in_specs, out_specs=out_specs, check_vma=False)
```

```python
import functools
import jax
import jax.numpy as jnp
from jax import lax
from jax.experimental import pallas as pl
from jax.experimental.pallas import tpu as pltpu
from jax.sharding import Mesh, PartitionSpec as P

decay_rate = 0.9
step_size = 0.05
clip_level = 1.0
tiny_square = 1e-30
ROW = ("x", "core")
COL = ("y", "z")


def shift(value, axis, by):
    n = lax.axis_size(axis)
    return lax.ppermute(value, axis, [(i, (i + by) % n) for i in range(n)])


def pair_sum(value, axis, bit):
    n = lax.axis_size(axis)
    return value + lax.ppermute(value, axis, [(i, i ^ bit) for i in range(n)])


def spread_sum(value, axis):
    copies = jnp.broadcast_to(value[None], (lax.axis_size(axis),) + value.shape)
    return jnp.sum(lax.all_to_all(copies, axis, 0, 0, tiled=True), axis=0)


def gather4(value, axis):
    return shift(value, axis, 1), shift(value, axis, -1)


def share_kernel(n_core, place, source, target, done):
    n_z, n_y, part, half = target.shape
    top = pl.multiple_of(place[0] * part, part)
    copies = []
    for j in range(n_y):
        for i in range(n_z):
            block = (place[2] + j) % n_y * n_z + i
            left = pl.multiple_of((block * n_core + place[1]) * half, 128)
            copy = pltpu.make_async_copy(source.at[pl.ds(top, part), pl.ds(left, half)], target.at[i, j], done.at[i, j])
            copy.start()
            copies.append(copy)
    for copy in copies:
        copy.wait()


def share_out(place, out_grad, n_z, n_y, part, half, n_core):
    shape = (n_z, n_y, part, half)
    return pl.pallas_call(
        functools.partial(share_kernel, n_core),
        out_shape=jax.ShapeDtypeStruct(shape, out_grad.dtype),
        grid_spec=pltpu.PrefetchScalarGridSpec(
            num_scalar_prefetch=1,
            grid=(1,),
            in_specs=[pl.BlockSpec(memory_space=pl.ANY)],
            out_specs=pl.BlockSpec(shape, lambda i, place: (0, 0, 0, 0)),
            scratch_shapes=[pltpu.SemaphoreType.DMA((n_z, n_y))],
        ),
        compiler_params=pltpu.CompilerParams(vmem_limit_bytes=56 * 1024 * 1024),
        cost_estimate=pl.CostEstimate(flops=0, bytes_accessed=4 * n_z * n_y * part * half, transcendentals=0),
    )(place, out_grad)


def update_kernel(entries, entry_cols, place, sums, state, col_out, grad, weight, residual, new_weight, row_out, kept, given):
    rows, half = kept.shape
    rows_out = decay_rate * state[...] + (1.0 - decay_rate) * sums[0:8] / entry_cols
    upd = jnp.sum(jnp.sum(sums[8:16] / rows_out, axis=0, keepdims=True), axis=1, keepdims=True)
    upd_rms = jnp.sqrt(upd / entries)
    w_rms = jnp.sqrt(jnp.sum(sums[16:17], axis=1, keepdims=True) / entries)
    factor = step_size * w_rms / jnp.maximum(1.0, upd_rms / clip_level)
    row_out[...] = rows_out[0:1]
    scale = factor * lax.rsqrt(jnp.transpose(jnp.broadcast_to(rows_out[0:1], (8, rows)))[:, :1])
    for target, at in ((kept, place[1]), (given, 1 - place[1])):
        part = pl.ds(pl.multiple_of(at * half, 128), half)
        master = weight[:, part].astype(jnp.float32) + residual[:, part].astype(jnp.float32)
        delta = grad[:, part].astype(jnp.float32) * (scale * lax.rsqrt(col_out[:, part]))
        new = (master - delta).astype(jnp.bfloat16)
        target[...] = new
        new_weight[:, part] = new


def update(place, entries, entry_cols, sums, state, col_out, arrays, half):
    rows, cols = arrays[0].shape
    whole = lambda shape: pl.BlockSpec(shape, lambda i, place: (0,) * len(shape))
    return pl.pallas_call(
        functools.partial(update_kernel, entries, entry_cols),
        out_shape=(
            jax.ShapeDtypeStruct((rows, cols), jnp.bfloat16),
            jax.ShapeDtypeStruct((1, rows), jnp.float32),
            jax.ShapeDtypeStruct((rows, half), jnp.bfloat16),
            jax.ShapeDtypeStruct((rows, half), jnp.bfloat16),
        ),
        grid_spec=pltpu.PrefetchScalarGridSpec(
            num_scalar_prefetch=1,
            grid=(1,),
            in_specs=[whole(sums.shape), whole(state.shape), whole((1, cols))] + [whole((rows, cols))] * 3,
            out_specs=[whole((rows, cols)), whole((1, rows)), whole((rows, half)), whole((rows, half))],
        ),
        compiler_params=pltpu.CompilerParams(vmem_limit_bytes=16 * 1024 * 1024),
    )(place, sums, state, col_out, *arrays)


def product_kernel(*refs):
    weights, tokens, (mine, other) = refs[:8], refs[8:-2], refs[-2:]
    n_z, _, part, rows = mine.shape
    n_y, half = tokens[0].shape[1], tokens[0].shape[3]
    total = 0.0
    for j in range(n_y):
        weight = jnp.concatenate([weights[2 * j][...], weights[2 * j + 1][...]], axis=0)
        wide = jnp.concatenate([ref[:, j].reshape(ref.shape[0] * part, half) for ref in tokens], axis=0)
        total += lax.dot_general(wide, weight, (((1,), (1,)), ((), ())), preferred_element_type=jnp.float32)
    total = total.reshape(-1, n_z, part, 2 * rows)
    for n in range(total.shape[0]):
        mine[:, n] = total[n, :, :, :rows]
        other[:, n] = total[n, :, :, rows:]


def products(weights, n_z, *tokens):
    n_y, part, half = tokens[0].shape[1:]
    count = sum(t.shape[0] for t in tokens) // n_z
    rows = weights[0].shape[0]
    out = jax.ShapeDtypeStruct((n_z, count, part, rows), jnp.float32)
    return pl.pallas_call(
        product_kernel,
        out_shape=(out, out),
        in_specs=[pl.BlockSpec(memory_space=pltpu.VMEM)] * (8 + len(tokens)),
        out_specs=(pl.BlockSpec(memory_space=pltpu.VMEM),) * 2,
        compiler_params=pltpu.CompilerParams(vmem_limit_bytes=40 * 1024 * 1024),
        cost_estimate=pl.CostEstimate(
            flops=4 * n_z * count * part * rows * n_y * half,
            bytes_accessed=4 * n_y * rows * half + 2 * sum(t.size for t in tokens) + 8 * n_z * count * part * rows,
            transcendentals=0,
        ),
    )(*weights, *tokens)


def body(grad, weight, residual, row_state, col_state, out_grad):
    rows, cols = grad.shape
    tokens = out_grad.shape[0]
    n_x, n_core, n_y, n_z = (lax.axis_size(a) for a in ("x", "core", "y", "z"))
    x, core, y = (lax.axis_index(a) for a in ("x", "core", "y"))
    all_rows, all_cols = rows * n_x * n_core, cols * n_y * n_z
    part, half = tokens // n_x, cols // n_core

    place = jnp.stack([x, core, y]).astype(jnp.int32)
    share = share_out(place, out_grad, n_z, n_y, part, half, n_core)
    share = lax.all_to_all(share, "z", 0, 0, tiled=True)

    grad_full = grad.astype(jnp.float32)
    squares = grad_full * grad_full + tiny_square
    col_part = jnp.sum(squares, axis=0).reshape(cols // 128, 128)
    col_total = pair_sum(col_part, "core", 1)
    col_total = col_total + shift(col_total, "x", 1) + shift(col_total, "x", 2) + shift(col_total, "x", 3)
    col_out = decay_rate * col_state + (1.0 - decay_rate) * col_total.reshape(cols) / all_rows
    master = weight.astype(jnp.float32) + residual.astype(jnp.float32)
    row_part = jnp.sum(squares, axis=1)
    scaled_part = jnp.sum(grad_full * grad_full * (1.0 / col_out)[None, :], axis=1)
    w_part = jnp.sum(master * master, axis=1)
    four = jnp.stack([row_part, scaled_part, w_part, row_state])
    two = jnp.stack([four, shift(four, "core", 1)], axis=1)
    parts = jnp.concatenate([two, shift(two, "x", 1), shift(two, "x", 2), shift(two, "x", 3)], axis=1)
    w_sum = jnp.sum(parts[2], axis=0, keepdims=True)
    sums = jnp.concatenate([parts[0], parts[1], w_sum, jnp.zeros((7, rows), jnp.float32)])
    sums = pair_sum(pair_sum(sums, "y", 1), "y", 2)
    sums, share = lax.optimization_barrier((sums, share))
    before, after = gather4(share, "x")
    sums = pair_sum(pair_sum(pair_sum(sums, "z", 1), "z", 2), "z", 4)

    new_weight, row_out, kept, given = update(
        place, all_rows * all_cols, all_cols, sums, parts[3], col_out[None], (grad, weight, residual), half
    )
    taken = shift(given, "core", 1)
    kept_before, kept_after = gather4(kept, "y")
    kept_before, kept_after, before, after = lax.optimization_barrier((kept_before, kept_after, before, after))
    far_low = shift(before[: n_z // 2], "x", 1)
    far_high = shift(after[n_z // 2 :], "x", -1)
    taken_before, taken_after = gather4(taken, "y")
    kept_far = shift(kept_before, "y", 1)
    taken_far = shift(taken_after, "y", -1)
    weights = (kept, taken, kept_after, taken_after, kept_far, taken_far, kept_before, taken_before)
    first = products(weights, n_z, share, after, before)
    last = products(weights, n_z, far_low, far_high)
    total = jnp.concatenate([first[0] + shift(first[1], "core", 1), last[0] + shift(last[1], "core", 1)], axis=1)
    total = lax.all_to_all(total, "z", 0, 0, tiled=True)
    summed = jnp.sum(total, axis=0)
    summed = jnp.stack([summed[0], summed[1], summed[3], summed[2]])
    summed = lax.dynamic_slice_in_dim(jnp.concatenate([summed, summed]), (n_x - x) % n_x, n_x, 0)
    input_grad = summed.reshape(tokens, rows).astype(jnp.bfloat16)
    return (new_weight, row_out.reshape(rows), col_out, input_grad)


def solution(mesh):
    fine = Mesh(mesh.devices.reshape(4, 2, 4, 8), ("x", "core", "y", "z"))
    in_specs = (P(ROW, COL), P(ROW, COL), P(ROW, COL), P(ROW), P(COL), P(COL, None))
    out_specs = (P(ROW, COL), P(ROW), P(COL), P(COL, ROW))
    return jax.shard_map(body, mesh=fine, in_specs=in_specs, out_specs=out_specs, check_vma=False)
```

```python
import functools
import jax
import jax.numpy as jnp
from jax import lax
from jax.experimental import pallas as pl
from jax.experimental.pallas import tpu as pltpu
from jax.sharding import Mesh, PartitionSpec as P

decay_rate = 0.9
step_size = 0.05
clip_level = 1.0
tiny_square = 1e-30
ROW = ("x", "core")
COL = ("y", "z")


def shift(value, axis, by):
    n = lax.axis_size(axis)
    return lax.ppermute(value, axis, [(i, (i + by) % n) for i in range(n)])


def pair_sum(value, axis, bit):
    n = lax.axis_size(axis)
    return value + lax.ppermute(value, axis, [(i, i ^ bit) for i in range(n)])


def spread_sum(value, axis):
    copies = jnp.broadcast_to(value[None], (lax.axis_size(axis),) + value.shape)
    return jnp.sum(lax.all_to_all(copies, axis, 0, 0, tiled=True), axis=0)


def gather4(value, axis):
    return shift(value, axis, 1), shift(value, axis, -1)


def share_kernel(n_core, place, source, target, done):
    n_z, n_y, part, half = target.shape
    top = pl.multiple_of(place[0] * part, part)
    copies = []
    for j in range(n_y):
        for i in range(n_z):
            block = (place[2] + j) % n_y * n_z + i
            left = pl.multiple_of((block * n_core + place[1]) * half, 128)
            copy = pltpu.make_async_copy(source.at[pl.ds(top, part), pl.ds(left, half)], target.at[i, j], done.at[i, j])
            copy.start()
            copies.append(copy)
    for copy in copies:
        copy.wait()


def share_out(place, out_grad, n_z, n_y, part, half, n_core):
    shape = (n_z, n_y, part, half)
    return pl.pallas_call(
        functools.partial(share_kernel, n_core),
        out_shape=jax.ShapeDtypeStruct(shape, out_grad.dtype),
        grid_spec=pltpu.PrefetchScalarGridSpec(
            num_scalar_prefetch=1,
            grid=(1,),
            in_specs=[pl.BlockSpec(memory_space=pl.ANY)],
            out_specs=pl.BlockSpec(shape, lambda i, place: (0, 0, 0, 0)),
            scratch_shapes=[pltpu.SemaphoreType.DMA((n_z, n_y))],
        ),
        compiler_params=pltpu.CompilerParams(vmem_limit_bytes=56 * 1024 * 1024),
        cost_estimate=pl.CostEstimate(flops=0, bytes_accessed=4 * n_z * n_y * part * half, transcendentals=0),
    )(place, out_grad)


def update_kernel(entries, entry_cols, place, sums, state, col_out, grad, weight, residual, new_weight, row_out, kept, given):
    rows, half = kept.shape
    rows_out = decay_rate * state[...] + (1.0 - decay_rate) * sums[0:8] / entry_cols
    upd = jnp.sum(jnp.sum(sums[8:16] / rows_out, axis=0, keepdims=True), axis=1, keepdims=True)
    upd_rms = jnp.sqrt(upd / entries)
    w_rms = jnp.sqrt(jnp.sum(sums[16:17], axis=1, keepdims=True) / entries)
    factor = step_size * w_rms / jnp.maximum(1.0, upd_rms / clip_level)
    row_out[...] = rows_out[0:1]
    scale = factor * lax.rsqrt(jnp.transpose(jnp.broadcast_to(rows_out[0:1], (8, rows)))[:, :1])
    for target, at in ((kept, place[1]), (given, 1 - place[1])):
        part = pl.ds(pl.multiple_of(at * half, 128), half)
        master = weight[:, part].astype(jnp.float32) + residual[:, part].astype(jnp.float32)
        delta = grad[:, part].astype(jnp.float32) * (scale * lax.rsqrt(col_out[:, part]))
        new = (master - delta).astype(jnp.bfloat16)
        target[...] = new
        new_weight[:, part] = new


def update(place, entries, entry_cols, sums, state, col_out, arrays, half):
    rows, cols = arrays[0].shape
    whole = lambda shape: pl.BlockSpec(shape, lambda i, place: (0,) * len(shape))
    return pl.pallas_call(
        functools.partial(update_kernel, entries, entry_cols),
        out_shape=(
            jax.ShapeDtypeStruct((rows, cols), jnp.bfloat16),
            jax.ShapeDtypeStruct((1, rows), jnp.float32),
            jax.ShapeDtypeStruct((rows, half), jnp.bfloat16),
            jax.ShapeDtypeStruct((rows, half), jnp.bfloat16),
        ),
        grid_spec=pltpu.PrefetchScalarGridSpec(
            num_scalar_prefetch=1,
            grid=(1,),
            in_specs=[whole(sums.shape), whole(state.shape), whole((1, cols))] + [whole((rows, cols))] * 3,
            out_specs=[whole((rows, cols)), whole((1, rows)), whole((rows, half)), whole((rows, half))],
        ),
        compiler_params=pltpu.CompilerParams(vmem_limit_bytes=16 * 1024 * 1024),
    )(place, sums, state, col_out, *arrays)


def product_kernel(*refs):
    weights, tokens, (mine, other) = refs[:5], refs[5:-2], refs[-2:]
    n_z, _, part, rows = mine.shape
    n_y, half = tokens[0].shape[1], tokens[0].shape[3]
    own, after, far_low, far_high, before = (ref[...] for ref in weights)
    total = 0.0
    for j, weight in enumerate((own, after, jnp.concatenate([far_low, far_high], axis=0), before)):
        wide = jnp.concatenate([ref[:, j].reshape(ref.shape[0] * part, half) for ref in tokens], axis=0)
        total += lax.dot_general(wide, weight, (((1,), (1,)), ((), ())), preferred_element_type=jnp.float32)
    total = total.reshape(-1, n_z, part, 2 * rows)
    for n in range(total.shape[0]):
        mine[:, n] = total[n, :, :, :rows]
        other[:, n] = total[n, :, :, rows:]


def products(weights, n_z, *tokens):
    n_y, part, half = tokens[0].shape[1:]
    count = sum(t.shape[0] for t in tokens) // n_z
    rows = weights[0].shape[0] // 2
    out = jax.ShapeDtypeStruct((n_z, count, part, rows), jnp.float32)
    return pl.pallas_call(
        product_kernel,
        out_shape=(out, out),
        in_specs=[pl.BlockSpec(memory_space=pltpu.VMEM)] * (5 + len(tokens)),
        out_specs=(pl.BlockSpec(memory_space=pltpu.VMEM),) * 2,
        compiler_params=pltpu.CompilerParams(vmem_limit_bytes=40 * 1024 * 1024),
        cost_estimate=pl.CostEstimate(
            flops=4 * n_z * count * part * rows * n_y * half,
            bytes_accessed=4 * n_y * rows * half + 2 * sum(t.size for t in tokens) + 8 * n_z * count * part * rows,
            transcendentals=0,
        ),
    )(*weights, *tokens)


def body(grad, weight, residual, row_state, col_state, out_grad):
    rows, cols = grad.shape
    tokens = out_grad.shape[0]
    n_x, n_core, n_y, n_z = (lax.axis_size(a) for a in ("x", "core", "y", "z"))
    x, core, y = (lax.axis_index(a) for a in ("x", "core", "y"))
    all_rows, all_cols = rows * n_x * n_core, cols * n_y * n_z
    part, half = tokens // n_x, cols // n_core

    place = jnp.stack([x, core, y]).astype(jnp.int32)
    share = share_out(place, out_grad, n_z, n_y, part, half, n_core)
    share = lax.all_to_all(share, "z", 0, 0, tiled=True)

    grad_full = grad.astype(jnp.float32)
    squares = grad_full * grad_full + tiny_square
    col_part = jnp.sum(squares, axis=0).reshape(cols // 128, 128)
    col_total = pair_sum(col_part, "core", 1)
    col_total = col_total + shift(col_total, "x", 1) + shift(col_total, "x", 2) + shift(col_total, "x", 3)
    col_out = decay_rate * col_state + (1.0 - decay_rate) * col_total.reshape(cols) / all_rows
    master = weight.astype(jnp.float32) + residual.astype(jnp.float32)
    row_part = jnp.sum(squares, axis=1)
    scaled_part = jnp.sum(grad_full * grad_full * (1.0 / col_out)[None, :], axis=1)
    w_part = jnp.sum(master * master, axis=1)
    four = jnp.stack([row_part, scaled_part, w_part, row_state])
    two = jnp.stack([four, shift(four, "core", 1)], axis=1)
    parts = jnp.concatenate([two, shift(two, "x", 1), shift(two, "x", 2), shift(two, "x", 3)], axis=1)
    w_sum = jnp.sum(parts[2], axis=0, keepdims=True)
    sums = jnp.concatenate([parts[0], parts[1], w_sum, jnp.zeros((7, rows), jnp.float32)])
    sums = pair_sum(pair_sum(sums, "y", 1), "y", 2)
    sums, share = lax.optimization_barrier((sums, share))
    before, after = gather4(share, "x")
    sums = pair_sum(pair_sum(pair_sum(sums, "z", 1), "z", 2), "z", 4)

    new_weight, row_out, kept, given = update(
        place, all_rows * all_cols, all_cols, sums, parts[3], col_out[None], (grad, weight, residual), half
    )
    taken = shift(given, "core", 1)
    block = jnp.concatenate([kept, taken], axis=0)
    w_before, w_after = gather4(block, "y")
    far_low = shift(before[: n_z // 2], "x", 1)
    far_high = shift(after[n_z // 2 :], "x", -1)
    kept_far = shift(w_before[:rows], "y", 1)
    taken_far = shift(w_after[rows:], "y", -1)
    kept_far, taken_far, far_low, far_high = lax.optimization_barrier((kept_far, taken_far, far_low, far_high))
    weights = (block, w_after, kept_far, taken_far, w_before)
    first = products(weights, n_z, share, after, before)
    last = products(weights, n_z, far_low, far_high)
    total = jnp.concatenate([first[0] + shift(first[1], "core", 1), last[0] + shift(last[1], "core", 1)], axis=1)
    total = lax.all_to_all(total, "z", 0, 0, tiled=True)
    summed = jnp.sum(total, axis=0)
    summed = jnp.stack([summed[0], summed[1], summed[3], summed[2]])
    summed = lax.dynamic_slice_in_dim(jnp.concatenate([summed, summed]), (n_x - x) % n_x, n_x, 0)
    input_grad = summed.reshape(tokens, rows).astype(jnp.bfloat16)
    return (new_weight, row_out.reshape(rows), col_out, input_grad)


def solution(mesh):
    fine = Mesh(mesh.devices.reshape(4, 2, 4, 8), ("x", "core", "y", "z"))
    in_specs = (P(ROW, COL), P(ROW, COL), P(ROW, COL), P(ROW), P(COL), P(COL, None))
    out_specs = (P(ROW, COL), P(ROW), P(COL), P(COL, ROW))
    return jax.shard_map(body, mesh=fine, in_specs=in_specs, out_specs=out_specs, check_vma=False)
```

```python
import functools
import jax
import jax.numpy as jnp
from jax import lax
from jax.experimental import pallas as pl
from jax.experimental.pallas import tpu as pltpu
from jax.sharding import Mesh, PartitionSpec as P

decay_rate = 0.9
step_size = 0.05
clip_level = 1.0
tiny_square = 1e-30
ROW = ("x", "core")
COL = ("y", "z")


def shift(value, axis, by):
    n = lax.axis_size(axis)
    return lax.ppermute(value, axis, [(i, (i + by) % n) for i in range(n)])


def pair_sum(value, axis, bit):
    n = lax.axis_size(axis)
    return value + lax.ppermute(value, axis, [(i, i ^ bit) for i in range(n)])


def spread_sum(value, axis):
    copies = jnp.broadcast_to(value[None], (lax.axis_size(axis),) + value.shape)
    return jnp.sum(lax.all_to_all(copies, axis, 0, 0, tiled=True), axis=0)


def gather4(value, axis):
    return shift(value, axis, 1), shift(value, axis, -1)


def share_kernel(source, target, done):
    n_z, n_y, part, half = target.shape
    n_core = lax.axis_size("core")
    x, core, y = lax.axis_index("x"), lax.axis_index("core"), lax.axis_index("y")
    top = pl.multiple_of(x * part, part)
    copies = []
    for j in range(n_y):
        for i in range(n_z):
            block = (y + j) % n_y * n_z + i
            left = pl.multiple_of((block * n_core + core) * half, 128)
            copy = pltpu.make_async_copy(source.at[pl.ds(top, part), pl.ds(left, half)], target.at[i, j], done.at[i, j])
            copy.start()
            copies.append(copy)
    for copy in copies:
        copy.wait()


def share_out(out_grad, n_z, n_y, part, half):
    return pl.pallas_call(
        share_kernel,
        out_shape=jax.ShapeDtypeStruct((n_z, n_y, part, half), out_grad.dtype),
        in_specs=[pl.BlockSpec(memory_space=pltpu.HBM)],
        out_specs=pl.BlockSpec(memory_space=pltpu.VMEM),
        scratch_shapes=[pltpu.SemaphoreType.DMA((n_z, n_y))],
        compiler_params=pltpu.CompilerParams(vmem_limit_bytes=56 * 1024 * 1024),
        cost_estimate=pl.CostEstimate(flops=0, bytes_accessed=4 * n_z * n_y * part * half, transcendentals=0),
    )(out_grad)


def update_kernel(entries, entry_cols, sums, state, col_out, grad, weight, residual, new_weight, row_out, kept, given):
    rows, half = kept.shape
    rows_out = decay_rate * state[...] + (1.0 - decay_rate) * sums[0:8] / entry_cols
    upd = jnp.sum(jnp.sum(sums[8:16] / rows_out, axis=0, keepdims=True), axis=1, keepdims=True)
    upd_rms = jnp.sqrt(upd / entries)
    w_rms = jnp.sqrt(jnp.sum(sums[16:17], axis=1, keepdims=True) / entries)
    factor = step_size * w_rms / jnp.maximum(1.0, upd_rms / clip_level)
    row_out[...] = rows_out[0:1]
    scale = factor * lax.rsqrt(jnp.transpose(jnp.broadcast_to(rows_out[0:1], (8, rows)))[:, :1])
    core = lax.axis_index("core")
    for target, at in ((kept, core), (given, 1 - core)):
        part = pl.ds(pl.multiple_of(at * half, 128), half)
        master = weight[:, part].astype(jnp.float32) + residual[:, part].astype(jnp.float32)
        delta = grad[:, part].astype(jnp.float32) * (scale * lax.rsqrt(col_out[:, part]))
        new = (master - delta).astype(jnp.bfloat16)
        target[...] = new
        new_weight[:, part] = new


def update(entries, entry_cols, sums, state, col_out, arrays, half):
    rows, cols = arrays[0].shape
    vmem = pl.BlockSpec(memory_space=pltpu.VMEM)
    return pl.pallas_call(
        functools.partial(update_kernel, entries, entry_cols),
        out_shape=(
            jax.ShapeDtypeStruct((rows, cols), jnp.bfloat16),
            jax.ShapeDtypeStruct((1, rows), jnp.float32),
            jax.ShapeDtypeStruct((rows, half), jnp.bfloat16),
            jax.ShapeDtypeStruct((rows, half), jnp.bfloat16),
        ),
        in_specs=[vmem] * 6,
        out_specs=(vmem,) * 4,
        compiler_params=pltpu.CompilerParams(vmem_limit_bytes=16 * 1024 * 1024),
    )(sums, state, col_out, *arrays)


def joined(refs):
    return jnp.concatenate([ref[...] for ref in refs], axis=0)


def tokens_of(refs, j):
    return jnp.concatenate([ref[:, j].reshape(ref.shape[0] * ref.shape[2], ref.shape[3]) for ref in refs], axis=0)


def times(tokens, weights):
    return lax.dot_general(tokens, weights, (((1,), (1,)), ((), ())), preferred_element_type=jnp.float32)


def near_kernel(places, *refs):
    count = 2 * len(places)
    weights, tokens, total_ref = refs[:count], refs[count:-1], refs[-1]
    total = 0.0
    for n, j in enumerate(places):
        total += times(tokens_of(tokens, j), joined(weights[2 * n : 2 * n + 2]))
    total_ref[...] = total


def all_kernel(places, far, *refs):
    count = 2 * len(places)
    weights, far_weights, refs = refs[:count], refs[count : count + 2], refs[count + 2 :]
    tokens, far_tokens, partial, (mine, other) = refs[: len(places)], refs[len(places) : -3], refs[-3], refs[-2:]
    n_z, _, part, rows = mine.shape
    far_weight = joined(far_weights)
    near_total = partial[...] + times(tokens_of(tokens, far), far_weight)
    far_total = times(tokens_of(far_tokens, far), far_weight)
    for n, j in enumerate(places):
        far_total += times(tokens_of(far_tokens, j), joined(weights[2 * n : 2 * n + 2]))
    for place, total in enumerate([*near_total.reshape(-1, n_z, part, 2 * rows), far_total.reshape(n_z, part, 2 * rows)]):
        mine[:, place] = total[:, :, :rows]
        other[:, place] = total[:, :, rows:]


def near_products(weights, tokens, places):
    operands = [w for pair in weights for w in pair] + list(tokens)
    n_z, _, part, half = tokens[0].shape
    rows = weights[0][0].shape[0]
    shape = (len(tokens) * n_z * part, 2 * rows)
    return pl.pallas_call(
        functools.partial(near_kernel, places),
        out_shape=jax.ShapeDtypeStruct(shape, jnp.float32),
        in_specs=[pl.BlockSpec(memory_space=pltpu.VMEM)] * len(operands),
        out_specs=pl.BlockSpec(memory_space=pltpu.VMEM),
        compiler_params=pltpu.CompilerParams(vmem_limit_bytes=40 * 1024 * 1024),
        cost_estimate=pl.CostEstimate(
            flops=10 * shape[0] * shape[1] * len(places) * half,
            bytes_accessed=2 * sum(o.size for o in operands) + 4 * shape[0] * shape[1],
            transcendentals=0,
        ),
    )(*operands)


def all_products(weights, far_weights, tokens, far_tokens, partial, places):
    operands = [w for pair in weights for w in pair] + [*far_weights, *tokens, *far_tokens, partial]
    n_z, n_y, part, half = tokens[0].shape
    rows = far_weights[0].shape[0]
    out = jax.ShapeDtypeStruct((n_z, len(tokens) + 1, part, rows), jnp.float32)
    return pl.pallas_call(
        functools.partial(all_kernel, places, 2),
        out_shape=(out, out),
        in_specs=[pl.BlockSpec(memory_space=pltpu.VMEM)] * len(operands),
        out_specs=(pl.BlockSpec(memory_space=pltpu.VMEM),) * 2,
        compiler_params=pltpu.CompilerParams(vmem_limit_bytes=40 * 1024 * 1024),
        cost_estimate=pl.CostEstimate(
            flops=4 * (len(tokens) + n_y) * n_z * part * rows * half,
            bytes_accessed=2 * sum(o.size for o in operands),
            transcendentals=0,
        ),
    )(*operands)


def body(grad, weight, residual, row_state, col_state, out_grad):
    rows, cols = grad.shape
    tokens = out_grad.shape[0]
    n_x, n_core, n_y, n_z = (lax.axis_size(a) for a in ("x", "core", "y", "z"))
    x = lax.axis_index("x")
    all_rows, all_cols = rows * n_x * n_core, cols * n_y * n_z
    part, half = tokens // n_x, cols // n_core

    share = share_out(out_grad, n_z, n_y, part, half)
    share = lax.all_to_all(share, "z", 0, 0, tiled=True)

    grad_full = grad.astype(jnp.float32)
    squares = grad_full * grad_full + tiny_square
    col_part = jnp.sum(squares, axis=0).reshape(cols // 128, 128)
    col_total = pair_sum(col_part, "core", 1)
    col_total = col_total + shift(col_total, "x", 1) + shift(col_total, "x", 2) + shift(col_total, "x", 3)
    col_out = decay_rate * col_state + (1.0 - decay_rate) * col_total.reshape(cols) / all_rows
    master = weight.astype(jnp.float32) + residual.astype(jnp.float32)
    row_part = jnp.sum(squares, axis=1)
    scaled_part = jnp.sum(grad_full * grad_full * (1.0 / col_out)[None, :], axis=1)
    w_part = jnp.sum(master * master, axis=1)
    four = jnp.stack([row_part, scaled_part, w_part, row_state])
    two = jnp.stack([four, shift(four, "core", 1)], axis=1)
    parts = jnp.concatenate([two, shift(two, "x", 1), shift(two, "x", 2), shift(two, "x", 3)], axis=1)
    w_sum = jnp.sum(parts[2], axis=0, keepdims=True)
    sums = jnp.concatenate([parts[0], parts[1], w_sum, jnp.zeros((7, rows), jnp.float32)])
    sums = pair_sum(pair_sum(sums, "y", 1), "y", 2)
    sums = pair_sum(sums, "z", 1)
    sums, share = lax.optimization_barrier((sums, share))
    before, after = gather4(share, "x")
    sums = pair_sum(pair_sum(sums, "z", 2), "z", 4)

    new_weight, row_out, kept, given = update(
        all_rows * all_cols, all_cols, sums, parts[3], col_out[None], (grad, weight, residual), half
    )
    taken = shift(given, "core", 1)
    kept_before, taken_after = shift(kept, "y", 1), shift(taken, "y", -1)
    taken_before, kept_after = shift(taken, "y", 1), shift(kept, "y", -1)
    far_low = shift(before[: n_z // 2], "x", 1)
    far_high = shift(after[n_z // 2 :], "x", -1)
    kept_far = shift(kept_before, "y", 1)
    taken_far = shift(taken_after, "y", -1)
    kept_far, taken_far, far_low, far_high = lax.optimization_barrier((kept_far, taken_far, far_low, far_high))
    near_weights = ((kept, taken), (kept_after, taken_after), (kept_before, taken_before))
    near_tokens = (share, after, before)
    partial = near_products(near_weights, near_tokens, (0, 1, 3))
    mine, other = all_products(near_weights, (kept_far, taken_far), near_tokens, (far_low, far_high), partial, (0, 1, 3))
    total = mine + shift(other, "core", 1)
    total = lax.all_to_all(total, "z", 0, 0, tiled=True)
    summed = jnp.sum(total, axis=0)
    summed = jnp.stack([summed[0], summed[1], summed[3], summed[2]])
    summed = lax.dynamic_slice_in_dim(jnp.concatenate([summed, summed]), (n_x - x) % n_x, n_x, 0)
    input_grad = summed.reshape(tokens, rows).astype(jnp.bfloat16)
    return (new_weight, row_out.reshape(rows), col_out, input_grad)


def solution(mesh):
    fine = Mesh(mesh.devices.reshape(4, 2, 4, 8), ("x", "core", "y", "z"))
    in_specs = (P(ROW, COL), P(ROW, COL), P(ROW, COL), P(ROW), P(COL), P(COL, None))
    out_specs = (P(ROW, COL), P(ROW), P(COL), P(COL, ROW))
    return jax.shard_map(body, mesh=fine, in_specs=in_specs, out_specs=out_specs, check_vma=False)
```

```python
import functools
import jax
import jax.numpy as jnp
from jax import lax
from jax.experimental import pallas as pl
from jax.experimental.pallas import tpu as pltpu
from jax.sharding import Mesh, PartitionSpec as P

decay_rate = 0.9
step_size = 0.05
clip_level = 1.0
tiny_square = 1e-30
ROW = ("x", "core")
COL = ("y", "z")


def shift(value, axis, by):
    n = lax.axis_size(axis)
    return lax.ppermute(value, axis, [(i, (i + by) % n) for i in range(n)])


def pair_sum(value, axis, bit):
    n = lax.axis_size(axis)
    return value + lax.ppermute(value, axis, [(i, i ^ bit) for i in range(n)])


def swap(value, axis, bits):
    return lax.ppermute(value, axis, [(i, i ^ bits) for i in range(lax.axis_size(axis))])


def spread_sum(value, axis):
    copies = jnp.broadcast_to(value[None], (lax.axis_size(axis),) + value.shape)
    return jnp.sum(lax.all_to_all(copies, axis, 0, 0, tiled=True), axis=0)


def gather4(value, axis):
    return shift(value, axis, 1), shift(value, axis, -1)


def share_kernel(source, target, done):
    n_z, n_y, part, half = target.shape
    n_core = lax.axis_size("core")
    x, core, y = lax.axis_index("x"), lax.axis_index("core"), lax.axis_index("y")
    top = pl.multiple_of(x * part, part)
    copies = []
    for j in range(n_y):
        for i in range(n_z):
            block = (y + j) % n_y * n_z + i
            left = pl.multiple_of((block * n_core + core) * half, 128)
            copy = pltpu.make_async_copy(source.at[pl.ds(top, part), pl.ds(left, half)], target.at[i, j], done.at[i, j])
            copy.start()
            copies.append(copy)
    for copy in copies:
        copy.wait()


def share_out(out_grad, n_z, n_y, part, half):
    return pl.pallas_call(
        share_kernel,
        out_shape=jax.ShapeDtypeStruct((n_z, n_y, part, half), out_grad.dtype),
        in_specs=[pl.BlockSpec(memory_space=pltpu.HBM)],
        out_specs=pl.BlockSpec(memory_space=pltpu.VMEM),
        scratch_shapes=[pltpu.SemaphoreType.DMA((n_z, n_y))],
        compiler_params=pltpu.CompilerParams(vmem_limit_bytes=56 * 1024 * 1024),
        cost_estimate=pl.CostEstimate(flops=0, bytes_accessed=4 * n_z * n_y * part * half, transcendentals=0),
    )(out_grad)


def update_kernel(entries, entry_cols, sums, state, col_out, grad, weight, residual, new_weight, row_out, kept, given):
    rows, half = kept.shape
    rows_out = decay_rate * state[...] + (1.0 - decay_rate) * sums[0:8] / entry_cols
    upd = jnp.sum(jnp.sum(sums[8:16] / rows_out, axis=0, keepdims=True), axis=1, keepdims=True)
    upd_rms = jnp.sqrt(upd / entries)
    w_rms = jnp.sqrt(jnp.sum(sums[16:17], axis=1, keepdims=True) / entries)
    factor = step_size * w_rms / jnp.maximum(1.0, upd_rms / clip_level)
    row_out[...] = rows_out[0:1]
    scale = factor * lax.rsqrt(jnp.transpose(jnp.broadcast_to(rows_out[0:1], (8, rows)))[:, :1])
    core = lax.axis_index("core")
    for target, at in ((kept, core), (given, 1 - core)):
        part = pl.ds(pl.multiple_of(at * half, 128), half)
        master = weight[:, part].astype(jnp.float32) + residual[:, part].astype(jnp.float32)
        delta = grad[:, part].astype(jnp.float32) * (scale * lax.rsqrt(col_out[:, part]))
        new = (master - delta).astype(jnp.bfloat16)
        target[...] = new
        new_weight[:, part] = new


def update(entries, entry_cols, sums, state, col_out, arrays, half):
    rows, cols = arrays[0].shape
    vmem = pl.BlockSpec(memory_space=pltpu.VMEM)
    return pl.pallas_call(
        functools.partial(update_kernel, entries, entry_cols),
        out_shape=(
            jax.ShapeDtypeStruct((rows, cols), jnp.bfloat16),
            jax.ShapeDtypeStruct((1, rows), jnp.float32),
            jax.ShapeDtypeStruct((rows, half), jnp.bfloat16),
            jax.ShapeDtypeStruct((rows, half), jnp.bfloat16),
        ),
        in_specs=[vmem] * 6,
        out_specs=(vmem,) * 4,
        compiler_params=pltpu.CompilerParams(vmem_limit_bytes=16 * 1024 * 1024),
    )(sums, state, col_out, *arrays)


def joined(refs):
    return jnp.concatenate([ref[...] for ref in refs], axis=0)


def tokens_of(refs, j):
    return jnp.concatenate([ref[:, j].reshape(ref.shape[0] * ref.shape[2], ref.shape[3]) for ref in refs], axis=0)


def times(tokens, weights):
    return lax.dot_general(tokens, weights, (((1,), (1,)), ((), ())), preferred_element_type=jnp.float32)


def split_weights(sizes, refs):
    weights = []
    for size in sizes:
        weights.append(joined(refs[:size]))
        refs = refs[size:]
    return weights, refs


def near_kernel(sizes, places, *refs):
    weights, refs = split_weights(sizes, refs)
    tokens, total_ref = refs[:-1], refs[-1]
    total = 0.0
    for weight, j in zip(weights, places):
        total += times(tokens_of(tokens, j), weight)
    total_ref[...] = total


def all_kernel(sizes, places, far, *refs):
    (*weights, far_weight), refs = split_weights((*sizes, 2), refs)
    tokens, far_tokens, partial, (mine, other) = refs[:-5], refs[-5:-3], refs[-3], refs[-2:]
    n_z, _, part, rows = mine.shape
    near_total = partial[...] + times(tokens_of(tokens, far), far_weight)
    far_total = times(tokens_of(far_tokens, far), far_weight)
    for weight, j in zip(weights, places):
        far_total += times(tokens_of(far_tokens, j), weight)
    for place, total in enumerate([*near_total.reshape(-1, n_z, part, 2 * rows), far_total.reshape(n_z, part, 2 * rows)]):
        mine[:, place] = total[:, :, :rows]
        other[:, place] = total[:, :, rows:]


def near_products(weights, tokens, places):
    operands = [w for pair in weights for w in pair] + list(tokens)
    n_z, _, part, half = tokens[0].shape
    rows = weights[0][0].shape[0]
    shape = (len(tokens) * n_z * part, 2 * rows)
    return pl.pallas_call(
        functools.partial(near_kernel, tuple(map(len, weights)), places),
        out_shape=jax.ShapeDtypeStruct(shape, jnp.float32),
        in_specs=[pl.BlockSpec(memory_space=pltpu.VMEM)] * len(operands),
        out_specs=pl.BlockSpec(memory_space=pltpu.VMEM),
        compiler_params=pltpu.CompilerParams(vmem_limit_bytes=40 * 1024 * 1024),
        cost_estimate=pl.CostEstimate(
            flops=10 * shape[0] * shape[1] * len(places) * half,
            bytes_accessed=2 * sum(o.size for o in operands) + 4 * shape[0] * shape[1],
            transcendentals=0,
        ),
    )(*operands)


def all_products(weights, far_weights, tokens, far_tokens, partial, places):
    operands = [w for pair in weights for w in pair] + [*far_weights, *tokens, *far_tokens, partial]
    n_z, n_y, part, half = tokens[0].shape
    rows = far_weights[0].shape[0]
    out = jax.ShapeDtypeStruct((n_z, len(tokens) + 1, part, rows), jnp.float32)
    return pl.pallas_call(
        functools.partial(all_kernel, tuple(map(len, weights)), places, 2),
        out_shape=(out, out),
        in_specs=[pl.BlockSpec(memory_space=pltpu.VMEM)] * len(operands),
        out_specs=(pl.BlockSpec(memory_space=pltpu.VMEM),) * 2,
        compiler_params=pltpu.CompilerParams(vmem_limit_bytes=40 * 1024 * 1024),
        cost_estimate=pl.CostEstimate(
            flops=4 * (len(tokens) + n_y) * n_z * part * rows * half,
            bytes_accessed=2 * sum(o.size for o in operands),
            transcendentals=0,
        ),
    )(*operands)


def body(grad, weight, residual, row_state, col_state, out_grad):
    rows, cols = grad.shape
    tokens = out_grad.shape[0]
    n_x, n_core, n_y, n_z = (lax.axis_size(a) for a in ("x", "core", "y", "z"))
    x = lax.axis_index("x")
    all_rows, all_cols = rows * n_x * n_core, cols * n_y * n_z
    part, half = tokens // n_x, cols // n_core

    share = share_out(out_grad, n_z, n_y, part, half)
    share = lax.all_to_all(share, "z", 0, 0, tiled=True)

    grad_full = grad.astype(jnp.float32)
    squares = grad_full * grad_full + tiny_square
    col_part = jnp.sum(squares, axis=0).reshape(cols // 128, 128)
    col_total = pair_sum(col_part, "core", 1)
    col_total = col_total + shift(col_total, "x", 1) + shift(col_total, "x", 2) + shift(col_total, "x", 3)
    col_out = decay_rate * col_state + (1.0 - decay_rate) * col_total.reshape(cols) / all_rows
    master = weight.astype(jnp.float32) + residual.astype(jnp.float32)
    row_part = jnp.sum(squares, axis=1)
    scaled_part = jnp.sum(grad_full * grad_full * (1.0 / col_out)[None, :], axis=1)
    w_part = jnp.sum(master * master, axis=1)
    four = jnp.stack([row_part, scaled_part, w_part, row_state])
    two = jnp.stack([four, shift(four, "core", 1)], axis=1)
    parts = jnp.concatenate([two, shift(two, "x", 1), shift(two, "x", 2), shift(two, "x", 3)], axis=1)
    w_sum = jnp.sum(parts[2], axis=0, keepdims=True)
    sums = jnp.concatenate([parts[0], parts[1], w_sum, jnp.zeros((7, rows), jnp.float32)])
    sums = pair_sum(pair_sum(sums, "y", 1), "y", 2)
    sums = pair_sum(sums, "z", 1)
    sums, share = lax.optimization_barrier((sums, share))
    before, after = gather4(share, "x")
    sums = (sums + swap(sums, "z", 2)) + (swap(sums, "z", 4) + swap(sums, "z", 6))

    new_weight, row_out, kept, given = update(
        all_rows * all_cols, all_cols, sums, parts[3], col_out[None], (grad, weight, residual), half
    )
    taken = shift(given, "core", 1)
    w_before = shift(jnp.concatenate([kept, taken]), "y", 1)
    taken_after, kept_after = shift(taken, "y", -1), shift(kept, "y", -1)
    far_low = shift(before[: n_z // 2], "x", 1)
    far_high = shift(after[n_z // 2 :], "x", -1)
    kept_far = shift(w_before[:rows], "y", 1)
    taken_far = shift(taken_after, "y", -1)
    kept_far, taken_far, far_low, far_high = lax.optimization_barrier((kept_far, taken_far, far_low, far_high))
    near_weights = ((kept, taken), (kept_after, taken_after), (w_before,))
    near_tokens = (share, after, before)
    partial = near_products(near_weights, near_tokens, (0, 1, 3))
    mine, other = all_products(near_weights, (kept_far, taken_far), near_tokens, (far_low, far_high), partial, (0, 1, 3))
    total = mine + shift(other, "core", 1)
    total = lax.all_to_all(total, "z", 0, 0, tiled=True)
    summed = jnp.sum(total, axis=0)
    summed = jnp.stack([summed[0], summed[1], summed[3], summed[2]])
    summed = lax.dynamic_slice_in_dim(jnp.concatenate([summed, summed]), (n_x - x) % n_x, n_x, 0)
    input_grad = summed.reshape(tokens, rows).astype(jnp.bfloat16)
    return (new_weight, row_out.reshape(rows), col_out, input_grad)


def solution(mesh):
    fine = Mesh(mesh.devices.reshape(4, 2, 4, 8), ("x", "core", "y", "z"))
    in_specs = (P(ROW, COL), P(ROW, COL), P(ROW, COL), P(ROW), P(COL), P(COL, None))
    out_specs = (P(ROW, COL), P(ROW), P(COL), P(COL, ROW))
    return jax.shard_map(body, mesh=fine, in_specs=in_specs, out_specs=out_specs, check_vma=False)
```

```python
import functools
import jax
import jax.numpy as jnp
from jax import lax
from jax.experimental import pallas as pl
from jax.experimental.pallas import tpu as pltpu
from jax.sharding import Mesh, PartitionSpec as P

decay_rate = 0.9
step_size = 0.05
clip_level = 1.0
tiny_square = 1e-30
ROW = ("x", "core")
COL = ("y", "z")


def shift(value, axis, by):
    n = lax.axis_size(axis)
    return lax.ppermute(value, axis, [(i, (i + by) % n) for i in range(n)])


def pair_sum(value, axis, bit):
    n = lax.axis_size(axis)
    return value + lax.ppermute(value, axis, [(i, i ^ bit) for i in range(n)])


def swap(value, axis, bits):
    return lax.ppermute(value, axis, [(i, i ^ bits) for i in range(lax.axis_size(axis))])


def spread_sum(value, axis):
    copies = jnp.broadcast_to(value[None], (lax.axis_size(axis),) + value.shape)
    return jnp.sum(lax.all_to_all(copies, axis, 0, 0, tiled=True), axis=0)


def gather4(value, axis):
    return shift(value, axis, 1), shift(value, axis, -1)


def share_kernel(source, target, held, done, sent):
    n_z, n_y, part, half = target.shape
    n_core = lax.axis_size("core")
    x, core, y = lax.axis_index("x"), lax.axis_index("core"), lax.axis_index("y")
    top = pl.multiple_of(x * part, part)
    copies = []
    for i in range(n_z):
        for j in range(n_y):
            block = (y + j) % n_y * n_z + i
            left = pl.multiple_of((block * n_core + core) * half, 128)
            copy = pltpu.make_async_copy(source.at[pl.ds(top, part), pl.ds(left, half)], held.at[i, j], done.at[i, j])
            copy.start()
            copies.append(copy)
    out = []
    for i in range(n_z):
        for copy in copies[i * n_y : (i + 1) * n_y]:
            copy.wait()
        copy = pltpu.make_async_copy(held.at[i], target.at[i], sent.at[i])
        copy.start()
        out.append(copy)
    for copy in out:
        copy.wait()


def share_out(out_grad, n_z, n_y, part, half):
    return pl.pallas_call(
        share_kernel,
        out_shape=jax.ShapeDtypeStruct((n_z, n_y, part, half), out_grad.dtype),
        in_specs=[pl.BlockSpec(memory_space=pltpu.HBM)],
        out_specs=pl.BlockSpec(memory_space=pl.ANY),
        scratch_shapes=[
            pltpu.VMEM((n_z, n_y, part, half), out_grad.dtype),
            pltpu.SemaphoreType.DMA((n_z, n_y)),
            pltpu.SemaphoreType.DMA((n_z,)),
        ],
        compiler_params=pltpu.CompilerParams(vmem_limit_bytes=56 * 1024 * 1024),
        cost_estimate=pl.CostEstimate(flops=0, bytes_accessed=4 * n_z * n_y * part * half, transcendentals=0),
    )(out_grad)


def update_kernel(entries, entry_cols, sums, state, col_out, grad, weight, residual, new_weight, row_out, kept, given):
    rows, half = kept.shape
    rows_out = decay_rate * state[...] + (1.0 - decay_rate) * sums[0:8] / entry_cols
    upd = jnp.sum(jnp.sum(sums[8:16] / rows_out, axis=0, keepdims=True), axis=1, keepdims=True)
    upd_rms = jnp.sqrt(upd / entries)
    w_rms = jnp.sqrt(jnp.sum(sums[16:17], axis=1, keepdims=True) / entries)
    factor = step_size * w_rms / jnp.maximum(1.0, upd_rms / clip_level)
    row_out[...] = rows_out[0:1]
    scale = factor * lax.rsqrt(jnp.transpose(jnp.broadcast_to(rows_out[0:1], (8, rows)))[:, :1])
    core = lax.axis_index("core")
    for target, at in ((kept, core), (given, 1 - core)):
        part = pl.ds(pl.multiple_of(at * half, 128), half)
        master = weight[:, part].astype(jnp.float32) + residual[:, part].astype(jnp.float32)
        delta = grad[:, part].astype(jnp.float32) * (scale * lax.rsqrt(col_out[:, part]))
        new = (master - delta).astype(jnp.bfloat16)
        target[...] = new
        new_weight[:, part] = new


def update(entries, entry_cols, sums, state, col_out, arrays, half):
    rows, cols = arrays[0].shape
    vmem = pl.BlockSpec(memory_space=pltpu.VMEM)
    return pl.pallas_call(
        functools.partial(update_kernel, entries, entry_cols),
        out_shape=(
            jax.ShapeDtypeStruct((rows, cols), jnp.bfloat16),
            jax.ShapeDtypeStruct((1, rows), jnp.float32),
            jax.ShapeDtypeStruct((rows, half), jnp.bfloat16),
            jax.ShapeDtypeStruct((rows, half), jnp.bfloat16),
        ),
        in_specs=[vmem] * 6,
        out_specs=(vmem,) * 4,
        compiler_params=pltpu.CompilerParams(vmem_limit_bytes=16 * 1024 * 1024),
    )(sums, state, col_out, *arrays)


def joined(refs):
    return jnp.concatenate([ref[...] for ref in refs], axis=0)


def tokens_of(refs, j):
    return jnp.concatenate([ref[:, j].reshape(ref.shape[0] * ref.shape[2], ref.shape[3]) for ref in refs], axis=0)


def times(tokens, weights):
    return lax.dot_general(tokens, weights, (((1,), (1,)), ((), ())), preferred_element_type=jnp.float32)


def split_weights(sizes, refs):
    weights = []
    for size in sizes:
        weights.append(joined(refs[:size]))
        refs = refs[size:]
    return weights, refs


def near_kernel(sizes, places, *refs):
    weights, refs = split_weights(sizes, refs)
    tokens, total_ref = refs[:-1], refs[-1]
    total = 0.0
    for weight, j in zip(weights, places):
        total += times(tokens_of(tokens, j), weight)
    total_ref[...] = total


def all_kernel(sizes, places, far, *refs):
    (*weights, far_weight), refs = split_weights((*sizes, 2), refs)
    tokens, far_tokens, partial, (mine, other) = refs[:-5], refs[-5:-3], refs[-3], refs[-2:]
    n_z, _, part, rows = mine.shape
    near_total = partial[...] + times(tokens_of(tokens, far), far_weight)
    far_total = times(tokens_of(far_tokens, far), far_weight)
    for weight, j in zip(weights, places):
        far_total += times(tokens_of(far_tokens, j), weight)
    for place, total in enumerate([*near_total.reshape(-1, n_z, part, 2 * rows), far_total.reshape(n_z, part, 2 * rows)]):
        mine[:, place] = total[:, :, :rows]
        other[:, place] = total[:, :, rows:]


def near_products(weights, tokens, places):
    operands = [w for pair in weights for w in pair] + list(tokens)
    n_z, _, part, half = tokens[0].shape
    rows = weights[0][0].shape[0]
    shape = (len(tokens) * n_z * part, 2 * rows)
    return pl.pallas_call(
        functools.partial(near_kernel, tuple(map(len, weights)), places),
        out_shape=jax.ShapeDtypeStruct(shape, jnp.float32),
        in_specs=[pl.BlockSpec(memory_space=pltpu.VMEM)] * len(operands),
        out_specs=pl.BlockSpec(memory_space=pltpu.VMEM),
        compiler_params=pltpu.CompilerParams(vmem_limit_bytes=40 * 1024 * 1024),
        cost_estimate=pl.CostEstimate(
            flops=10 * shape[0] * shape[1] * len(places) * half,
            bytes_accessed=2 * sum(o.size for o in operands) + 4 * shape[0] * shape[1],
            transcendentals=0,
        ),
    )(*operands)


def all_products(weights, far_weights, tokens, far_tokens, partial, places):
    operands = [w for pair in weights for w in pair] + [*far_weights, *tokens, *far_tokens, partial]
    n_z, n_y, part, half = tokens[0].shape
    rows = far_weights[0].shape[0]
    out = jax.ShapeDtypeStruct((n_z, len(tokens) + 1, part, rows), jnp.float32)
    return pl.pallas_call(
        functools.partial(all_kernel, tuple(map(len, weights)), places, 2),
        out_shape=(out, out),
        in_specs=[pl.BlockSpec(memory_space=pltpu.VMEM)] * len(operands),
        out_specs=(pl.BlockSpec(memory_space=pltpu.VMEM),) * 2,
        compiler_params=pltpu.CompilerParams(vmem_limit_bytes=40 * 1024 * 1024),
        cost_estimate=pl.CostEstimate(
            flops=4 * (len(tokens) + n_y) * n_z * part * rows * half,
            bytes_accessed=2 * sum(o.size for o in operands),
            transcendentals=0,
        ),
    )(*operands)


def body(grad, weight, residual, row_state, col_state, out_grad):
    rows, cols = grad.shape
    tokens = out_grad.shape[0]
    n_x, n_core, n_y, n_z = (lax.axis_size(a) for a in ("x", "core", "y", "z"))
    x = lax.axis_index("x")
    all_rows, all_cols = rows * n_x * n_core, cols * n_y * n_z
    part, half = tokens // n_x, cols // n_core

    share = share_out(out_grad, n_z, n_y, part, half)
    share = lax.all_to_all(share, "z", 0, 0, tiled=True)

    grad_full = grad.astype(jnp.float32)
    squares = grad_full * grad_full + tiny_square
    col_part = jnp.sum(squares, axis=0).reshape(cols // 128, 128)
    col_total = pair_sum(col_part, "core", 1)
    col_total = col_total + shift(col_total, "x", 1) + shift(col_total, "x", 2) + shift(col_total, "x", 3)
    col_out = decay_rate * col_state + (1.0 - decay_rate) * col_total.reshape(cols) / all_rows
    master = weight.astype(jnp.float32) + residual.astype(jnp.float32)
    row_part = jnp.sum(squares, axis=1)
    scaled_part = jnp.sum(grad_full * grad_full * (1.0 / col_out)[None, :], axis=1)
    w_part = jnp.sum(master * master, axis=1)
    four = jnp.stack([row_part, scaled_part, w_part, row_state])
    two = jnp.stack([four, shift(four, "core", 1)], axis=1)
    parts = jnp.concatenate([two, shift(two, "x", 1), shift(two, "x", 2), shift(two, "x", 3)], axis=1)
    w_sum = jnp.sum(parts[2], axis=0, keepdims=True)
    sums = jnp.concatenate([parts[0], parts[1], w_sum, jnp.zeros((7, rows), jnp.float32)])
    sums = pair_sum(pair_sum(sums, "y", 1), "y", 2)
    sums = pair_sum(sums, "z", 1)
    sums, share = lax.optimization_barrier((sums, share))
    before, after = gather4(share, "x")
    sums = (sums + swap(sums, "z", 2)) + (swap(sums, "z", 4) + swap(sums, "z", 6))

    new_weight, row_out, kept, given = update(
        all_rows * all_cols, all_cols, sums, parts[3], col_out[None], (grad, weight, residual), half
    )
    taken = shift(given, "core", 1)
    w_before = shift(jnp.concatenate([kept, taken]), "y", 1)
    taken_after, kept_after = shift(taken, "y", -1), shift(kept, "y", -1)
    far_low = shift(before[: n_z // 2], "x", 1)
    far_high = shift(after[n_z // 2 :], "x", -1)
    kept_far = shift(w_before[:rows], "y", 1)
    taken_far = shift(taken_after, "y", -1)
    kept_far, taken_far, far_low, far_high = lax.optimization_barrier((kept_far, taken_far, far_low, far_high))
    near_weights = ((kept, taken), (kept_after, taken_after), (w_before,))
    near_tokens = (share, after, before)
    partial = near_products(near_weights, near_tokens, (0, 1, 3))
    mine, other = all_products(near_weights, (kept_far, taken_far), near_tokens, (far_low, far_high), partial, (0, 1, 3))
    total = mine + shift(other, "core", 1)
    total = lax.all_to_all(total, "z", 0, 0, tiled=True)
    summed = jnp.sum(total, axis=0)
    summed = jnp.stack([summed[0], summed[1], summed[3], summed[2]])
    summed = lax.dynamic_slice_in_dim(jnp.concatenate([summed, summed]), (n_x - x) % n_x, n_x, 0)
    input_grad = summed.reshape(tokens, rows).astype(jnp.bfloat16)
    return (new_weight, row_out.reshape(rows), col_out, input_grad)


def solution(mesh):
    fine = Mesh(mesh.devices.reshape(4, 2, 4, 8), ("x", "core", "y", "z"))
    in_specs = (P(ROW, COL), P(ROW, COL), P(ROW, COL), P(ROW), P(COL), P(COL, None))
    out_specs = (P(ROW, COL), P(ROW), P(COL), P(COL, ROW))
    return jax.shard_map(body, mesh=fine, in_specs=in_specs, out_specs=out_specs, check_vma=False)
```

```python
import functools
import jax
import jax.numpy as jnp
from jax import lax
from jax.experimental import pallas as pl
from jax.experimental.pallas import tpu as pltpu
from jax.sharding import Mesh, PartitionSpec as P

decay_rate = 0.9
step_size = 0.05
clip_level = 1.0
tiny_square = 1e-30
ROW = ("x", "core")
COL = ("y", "z")


def shift(value, axis, by):
    n = lax.axis_size(axis)
    return lax.ppermute(value, axis, [(i, (i + by) % n) for i in range(n)])


def pair_sum(value, axis, bit):
    n = lax.axis_size(axis)
    return value + lax.ppermute(value, axis, [(i, i ^ bit) for i in range(n)])


def swap(value, axis, bits):
    return lax.ppermute(value, axis, [(i, i ^ bits) for i in range(lax.axis_size(axis))])


def spread_sum(value, axis):
    copies = jnp.broadcast_to(value[None], (lax.axis_size(axis),) + value.shape)
    return jnp.sum(lax.all_to_all(copies, axis, 0, 0, tiled=True), axis=0)


def gather4(value, axis):
    return shift(value, axis, 1), shift(value, axis, -1)


def share_kernel(source, target, held, done, sent):
    n_z, n_y, part, half = target.shape
    n_core = lax.axis_size("core")
    x, core, y = lax.axis_index("x"), lax.axis_index("core"), lax.axis_index("y")
    top = pl.multiple_of(x * part, part)
    copies = []
    for i in range(n_z):
        for j in range(n_y):
            block = (y + j) % n_y * n_z + i
            left = pl.multiple_of((block * n_core + core) * half, 128)
            copy = pltpu.make_async_copy(source.at[pl.ds(top, part), pl.ds(left, half)], held.at[i, j], done.at[i, j])
            copy.start()
            copies.append(copy)
    out = []
    for i in range(n_z):
        for copy in copies[i * n_y : (i + 1) * n_y]:
            copy.wait()
        copy = pltpu.make_async_copy(held.at[i], target.at[i], sent.at[i])
        copy.start()
        out.append(copy)
    for copy in out:
        copy.wait()


def share_out(out_grad, n_z, n_y, part, half):
    return pl.pallas_call(
        share_kernel,
        out_shape=jax.ShapeDtypeStruct((n_z, n_y, part, half), out_grad.dtype),
        in_specs=[pl.BlockSpec(memory_space=pltpu.HBM)],
        out_specs=pl.BlockSpec(memory_space=pl.ANY),
        scratch_shapes=[
            pltpu.VMEM((n_z, n_y, part, half), out_grad.dtype),
            pltpu.SemaphoreType.DMA((n_z, n_y)),
            pltpu.SemaphoreType.DMA((n_z,)),
        ],
        compiler_params=pltpu.CompilerParams(vmem_limit_bytes=56 * 1024 * 1024),
        cost_estimate=pl.CostEstimate(flops=0, bytes_accessed=4 * n_z * n_y * part * half, transcendentals=0),
    )(out_grad)


def update_kernel(entries, entry_cols, sums, state, col_out, grad, weight, residual, new_weight, row_out, kept, given):
    rows, half = kept.shape
    rows_out = decay_rate * state[...] + (1.0 - decay_rate) * sums[0:8] / entry_cols
    upd = jnp.sum(jnp.sum(sums[8:16] / rows_out, axis=0, keepdims=True), axis=1, keepdims=True)
    upd_rms = jnp.sqrt(upd / entries)
    w_rms = jnp.sqrt(jnp.sum(sums[16:17], axis=1, keepdims=True) / entries)
    factor = step_size * w_rms / jnp.maximum(1.0, upd_rms / clip_level)
    row_out[...] = rows_out[0:1]
    scale = factor * lax.rsqrt(jnp.transpose(jnp.broadcast_to(rows_out[0:1], (8, rows)))[:, :1])
    core = lax.axis_index("core")
    for target, at in ((kept, core), (given, 1 - core)):
        part = pl.ds(pl.multiple_of(at * half, 128), half)
        master = weight[:, part].astype(jnp.float32) + residual[:, part].astype(jnp.float32)
        delta = grad[:, part].astype(jnp.float32) * (scale * lax.rsqrt(col_out[:, part]))
        new = (master - delta).astype(jnp.bfloat16)
        target[...] = new
        new_weight[:, part] = new


def update(entries, entry_cols, sums, state, col_out, arrays, half):
    rows, cols = arrays[0].shape
    vmem = pl.BlockSpec(memory_space=pltpu.VMEM)
    return pl.pallas_call(
        functools.partial(update_kernel, entries, entry_cols),
        out_shape=(
            jax.ShapeDtypeStruct((rows, cols), jnp.bfloat16),
            jax.ShapeDtypeStruct((1, rows), jnp.float32),
            jax.ShapeDtypeStruct((rows, half), jnp.bfloat16),
            jax.ShapeDtypeStruct((rows, half), jnp.bfloat16),
        ),
        in_specs=[vmem] * 6,
        out_specs=(vmem,) * 4,
        compiler_params=pltpu.CompilerParams(vmem_limit_bytes=16 * 1024 * 1024),
        cost_estimate=pl.CostEstimate(flops=rows * cols, bytes_accessed=rows * cols, transcendentals=0),
    )(sums, state, col_out, *arrays)


def joined(refs):
    return jnp.concatenate([ref[...] for ref in refs], axis=0)


def tokens_of(refs, j):
    return jnp.concatenate([ref[:, j].reshape(ref.shape[0] * ref.shape[2], ref.shape[3]) for ref in refs], axis=0)


def times(tokens, weights):
    return lax.dot_general(tokens, weights, (((1,), (1,)), ((), ())), preferred_element_type=jnp.float32)


def split_weights(sizes, refs):
    weights = []
    for size in sizes:
        weights.append(joined(refs[:size]))
        refs = refs[size:]
    return weights, refs


def near_kernel(sizes, places, *refs):
    weights, refs = split_weights(sizes, refs)
    tokens, total_ref = refs[:-1], refs[-1]
    total = 0.0
    for weight, j in zip(weights, places):
        total += times(tokens_of(tokens, j), weight)
    total_ref[...] = total


def far_kernel(sizes, places, far, *refs):
    (*weights, far_weight), refs = split_weights((*sizes, 2), refs)
    tokens, (mine, other) = refs[:2], refs[2:]
    n_z, part, rows = mine.shape
    total = times(tokens_of(tokens, far), far_weight)
    for weight, j in zip(weights, places):
        total += times(tokens_of(tokens, j), weight)
    total = total.reshape(n_z, part, 2 * rows)
    mine[...], other[...] = total[:, :, :rows], total[:, :, rows:]


def rest_kernel(far, *refs):
    weight, tokens, partial, (mine, other) = joined(refs[:2]), refs[2:-3], refs[-3], refs[-2:]
    n_z, _, part, rows = mine.shape
    total = (partial[...] + times(tokens_of(tokens, far), weight)).reshape(-1, n_z, part, 2 * rows)
    for place in range(total.shape[0]):
        mine[:, place] = total[place, :, :, :rows]
        other[:, place] = total[place, :, :, rows:]


def near_products(weights, tokens, places):
    operands = [w for pair in weights for w in pair] + list(tokens)
    n_z, _, part, half = tokens[0].shape
    rows = weights[0][0].shape[0]
    shape = (len(tokens) * n_z * part, 2 * rows)
    return pl.pallas_call(
        functools.partial(near_kernel, tuple(map(len, weights)), places),
        out_shape=jax.ShapeDtypeStruct(shape, jnp.float32),
        in_specs=[pl.BlockSpec(memory_space=pltpu.VMEM)] * len(operands),
        out_specs=pl.BlockSpec(memory_space=pltpu.VMEM),
        compiler_params=pltpu.CompilerParams(vmem_limit_bytes=40 * 1024 * 1024),
        cost_estimate=pl.CostEstimate(
            flops=10 * shape[0] * shape[1] * len(places) * half,
            bytes_accessed=2 * sum(o.size for o in operands) + 4 * shape[0] * shape[1],
            transcendentals=0,
        ),
    )(*operands)


def pair_call(kernel, shape, flops, operands):
    out = jax.ShapeDtypeStruct(shape, jnp.float32)
    return pl.pallas_call(
        kernel,
        out_shape=(out, out),
        in_specs=[pl.BlockSpec(memory_space=pltpu.VMEM)] * len(operands),
        out_specs=(pl.BlockSpec(memory_space=pltpu.VMEM),) * 2,
        compiler_params=pltpu.CompilerParams(vmem_limit_bytes=40 * 1024 * 1024),
        cost_estimate=pl.CostEstimate(
            flops=flops, bytes_accessed=2 * sum(o.size for o in operands), transcendentals=0
        ),
    )(*operands)


def body(grad, weight, residual, row_state, col_state, out_grad):
    rows, cols = grad.shape
    tokens = out_grad.shape[0]
    n_x, n_core, n_y, n_z = (lax.axis_size(a) for a in ("x", "core", "y", "z"))
    x = lax.axis_index("x")
    all_rows, all_cols = rows * n_x * n_core, cols * n_y * n_z
    part, half = tokens // n_x, cols // n_core

    share = share_out(out_grad, n_z, n_y, part, half)
    share = lax.all_to_all(share, "z", 0, 0, tiled=True)

    grad_full = grad.astype(jnp.float32)
    squares = grad_full * grad_full + tiny_square
    col_part = jnp.sum(squares, axis=0).reshape(cols // 128, 128)
    col_total = pair_sum(col_part, "core", 1)
    col_total = col_total + shift(col_total, "x", 1) + shift(col_total, "x", 2) + shift(col_total, "x", 3)
    col_out = decay_rate * col_state + (1.0 - decay_rate) * col_total.reshape(cols) / all_rows
    master = weight.astype(jnp.float32) + residual.astype(jnp.float32)
    row_part = jnp.sum(squares, axis=1)
    scaled_part = jnp.sum(grad_full * grad_full * (1.0 / col_out)[None, :], axis=1)
    w_part = jnp.sum(master * master, axis=1)
    four = jnp.stack([row_part, scaled_part, w_part, row_state])
    two = jnp.stack([four, shift(four, "core", 1)], axis=1)
    parts = jnp.concatenate([two, shift(two, "x", 1), shift(two, "x", 2), shift(two, "x", 3)], axis=1)
    w_sum = jnp.sum(parts[2], axis=0, keepdims=True)
    sums = jnp.concatenate([parts[0], parts[1], w_sum, jnp.zeros((7, rows), jnp.float32)])
    sums = pair_sum(pair_sum(sums, "y", 1), "y", 2)
    sums = pair_sum(sums, "z", 1)
    sums, share = lax.optimization_barrier((sums, share))
    before, after = gather4(share, "x")
    sums = (sums + swap(sums, "z", 2)) + (swap(sums, "z", 4) + swap(sums, "z", 6))

    new_weight, row_out, kept, given = update(
        all_rows * all_cols, all_cols, sums, parts[3], col_out[None], (grad, weight, residual), half
    )
    taken = shift(given, "core", 1)
    w_before, w_after = gather4(jnp.concatenate([kept, taken]), "y")
    far_low = shift(before[: n_z // 2], "x", 1)
    far_high = shift(after[n_z // 2 :], "x", -1)
    kept_far = shift(w_before[:rows], "y", 1)
    taken_far = shift(w_after[rows:], "y", -1)
    kept_far, taken_far, far_low, far_high = lax.optimization_barrier((kept_far, taken_far, far_low, far_high))
    near_weights = ((kept, taken), (w_after,), (w_before,))
    near_tokens = (share, after, before)
    partial = near_products(near_weights, near_tokens, (0, 1, 3))
    shape = (n_z, 3, part, rows)
    work = 4 * n_z * part * rows * half
    rest = pair_call(functools.partial(rest_kernel, 2), shape, 3 * work, [kept_far, taken_far, *near_tokens, partial])
    sizes = tuple(map(len, near_weights))
    flat = [w for group in near_weights for w in group]
    last = pair_call(
        functools.partial(far_kernel, sizes, (0, 1, 3), 2),
        (n_z, part, rows),
        n_y * work,
        [*flat, kept_far, taken_far, far_low, far_high],
    )
    rest = rest[0] + shift(rest[1], "core", 1)
    last = last[0] + shift(last[1], "core", 1)
    total = jnp.concatenate([rest, last[:, None]], axis=1)
    total = lax.all_to_all(total, "z", 0, 0, tiled=True)
    summed = jnp.sum(total, axis=0)
    summed = jnp.stack([summed[0], summed[1], summed[3], summed[2]])
    summed = lax.dynamic_slice_in_dim(jnp.concatenate([summed, summed]), (n_x - x) % n_x, n_x, 0)
    input_grad = summed.reshape(tokens, rows).astype(jnp.bfloat16)
    return (new_weight, row_out.reshape(rows), col_out, input_grad)


def solution(mesh):
    fine = Mesh(mesh.devices.reshape(4, 2, 4, 8), ("x", "core", "y", "z"))
    in_specs = (P(ROW, COL), P(ROW, COL), P(ROW, COL), P(ROW), P(COL), P(COL, None))
    out_specs = (P(ROW, COL), P(ROW), P(COL), P(COL, ROW))
    return jax.shard_map(body, mesh=fine, in_specs=in_specs, out_specs=out_specs, check_vma=False)
```
